256 devices in a mesh: gx: 32 (over y, x, core), gy: 8 (over z).
Axes of the slice: x: 4, y: 4, z: 8, core: 2. Of those that a mesh axis runs over, the one named last changes fastest.
Arguments:
- wave_coeffs: bfloat16 [1536, 131072], P('gy', 'gx'), may hold values from -6 to 6
- projectors: bfloat16 [1024, 131072], P(None, 'gx'), may hold values from -0.03125 to 0.03125
- miller_index: int32 [3, 131072], P(None, 'gx'), may hold values from -32 to 31, as said below
- occupations: float32 [1536], P('gy'), may hold values from 0 to 2
- species_map: int32 [128], replicated, may hold values from 0 to 3
- proj_counts: int32 [128], replicated, may hold values from 1 to 8, as said below
- onsite_base: float32 [4, 8, 8], replicated, may hold values from -5 to 5
Outputs:
- new_bands: float32 [1536, 131072], P('gy', 'gx')
The draws below stay inside these ranges and needn't reach their ends.
Inputs may be any that keep to these rules, and one draw needn't show every extreme that they name: `miller_index`: each column is a distinct lattice vector; columns run through whole shells of equal squared length in increasing order, the last shell possibly in part. `proj_counts`: some atom has exactly 8 projectors and some atom exactly one.
All inputs are finite; a program needn't handle non-finite values.
Results may differ from the reference program's by a relative error of at most 0.0031.
Values may be sent and summed in bfloat16 or wider, within the bound.
A program may use at most 64 MiB of HBM per device.

```python
import math
import jax
import jax.numpy as jnp
import numpy as np
from jax import lax

G = 131072
PMAX = 8
SPECIES = 4
ITERS = 2
BANDS = 1536
ATOMS = 128


def draw_miller_index(key, part):
    cube_side = 64
    cube_cells = jnp.arange(cube_side * cube_side * cube_side, dtype=jnp.int32)
    first_axis = cube_cells // (cube_side * cube_side) - 32
    second_axis = cube_cells // cube_side % cube_side - 32
    third_axis = cube_cells % cube_side - 32
    radius_sq = first_axis * first_axis + second_axis * second_axis + third_axis * third_axis
    shuffle = jax.random.permutation(jax.random.fold_in(key, 7), cube_side * cube_side * cube_side).astype(jnp.int32)
    scores = radius_sq * (cube_side * cube_side * cube_side) + shuffle
    sorted_cells = jnp.argsort(scores)[:G]
    return jnp.stack([first_axis[sorted_cells], second_axis[sorted_cells], third_axis[sorted_cells]]).astype(jnp.int32)


def draw_proj_counts(key, part):
    base_draw = jax.random.randint(jax.random.fold_in(key, 3), (ATOMS,), 2, PMAX + 1).astype(jnp.int32)
    placed = jax.random.permutation(jax.random.fold_in(key, 5), ATOMS)
    return base_draw.at[placed[0]].set(PMAX).at[placed[1]].set(1).astype(jnp.int32)


def place_ends(values, rng, smallest, high):
    place = [jax.random.randint(jax.random.fold_in(rng, axis), (), 0, length) for axis, length in enumerate(values.shape)]
    main_axis = values.shape.index(max(values.shape))
    next_to = place[:main_axis] + [(place[main_axis] + 1) % values.shape[main_axis]] + place[main_axis + 1:]
    return values.at[tuple(place)].set(smallest).at[tuple(next_to)].set(high)


def spiked(values, rng, source, target, parts, factor):
    owner, partner = [(jnp.arange(values.shape[axis_at]) // (values.shape[axis_at] // parts)).reshape([-1 if axis == axis_at else 1 for axis in range(values.ndim)]) for axis_at in (source, target)]
    chosen = jax.random.permutation(rng, parts)[partner]
    strong = (owner == chosen) | (owner == (partner + parts // 2) % parts)
    return jnp.where(strong, factor * values, values)


def shard_levels(own_key, extent, shards, smallest, largest):
    level, own = 1.0, jax.random.fold_in(own_key, 6)
    for axis_at, shards_of in shards:
        steps = jnp.exp(jax.random.uniform(jax.random.fold_in(own, axis_at), (shards_of,), jnp.float32, smallest / len(shards), largest / len(shards)))
        level = level * jnp.repeat(steps, extent[axis_at] // shards_of).reshape([-1 if axis == axis_at else 1 for axis in range(len(extent))])
    return level


def rank_bounds(count, slope):
    portions = [(1 << 20) // math.isqrt(standing ** slope) + 1 for standing in range(1, count + 1)]
    spread = 1 + sum(portions) // (1 << 30)
    return np.cumsum(np.array([max(1, weight // spread) for weight in portions]))


def skewed_ids(own_key, dims, count, skew):
    grid = rank_bounds(count, skew)
    lot = jax.random.randint(jax.random.fold_in(own_key, 1), dims, 0, int(grid[count - 1]))
    standing = jnp.searchsorted(jnp.asarray(grid, jnp.int32), lot, side="right")
    return jax.random.permutation(jax.random.fold_in(own_key, 2), count)[standing].astype(jnp.int32)


def scatter_about(key, extent, scale, most, pieces=(), held_as=jnp.bfloat16):
    drawn = jax.random.normal(key, extent, jnp.float32) * scale
    if len(pieces) > 0:
        drawn = shard_levels(key, extent, pieces, -0.22, 0.18) * drawn
    return jnp.clip(drawn, min=-most, max=most).astype(held_as)


def heavy_noise(key, extent, deviation, limit, cuts, heavy, kind=jnp.bfloat16):
    entries = deviation * jax.random.normal(key, extent, jnp.float32)
    if cuts:
        entries = entries * shard_levels(key, extent, cuts, -0.22, 0.18)
    return jnp.clip(spiked(entries, jax.random.fold_in(key, 3), *heavy), -limit, limit).astype(kind)


def setup_inputs(seed: int = 0) -> dict:
    seeds = jax.random.split(jax.random.key(seed), 8)
    return {
        "wave_coeffs": scatter_about(seeds[0], (BANDS, G), 1.0, 6.0, ((0, 8), (1, 32))),
        "projectors": heavy_noise(seeds[1], (ATOMS * PMAX, G), G ** -0.5, 0.03125, ((1, 32),), (1, 0, 32, 2.75)),
        "miller_index": draw_miller_index(jax.random.fold_in(seeds[7], 71), 0),
        "occupations": jnp.clip(2.0 * jax.random.uniform(seeds[3], (BANDS,), jnp.float32) ** shard_levels(seeds[3], (BANDS,), ((0, 8),), -0.2, 0.2), 0.0, 2.0),
        "species_map": place_ends(skewed_ids(seeds[4], (ATOMS,), SPECIES, 2), jax.random.fold_in(seeds[4], 3), 0, SPECIES - 1).astype(jnp.int32),
        "proj_counts": draw_proj_counts(jax.random.fold_in(seeds[7], 71), 0),
        "onsite_base": scatter_about(seeds[6], (SPECIES, PMAX, PMAX), 1.0, 5.0, (), jnp.float32),
    }


kinetic_unit = 1.0 / 600.0
hubbard_weight = 2.0
step_length = 0.5


def kinetic_of(miller_index):
    components = miller_index.astype(jnp.float32)
    metric = jnp.array([1.5, 1.0, 0.5], dtype=jnp.float32)
    return jnp.sum(metric[:, None] * components * components, axis=0) * kinetic_unit


def teter_factor(kinetic, band_kinetic):
    scaled_kinetic = kinetic[None, :] / band_kinetic[:, None]
    numerator = 27.0 + scaled_kinetic * (18.0 + scaled_kinetic * (12.0 + 8.0 * scaled_kinetic))
    return numerator / (numerator + 16.0 * scaled_kinetic ** 4)


def onsite_apply(raw_proj, occupations, species_map, proj_counts, onsite_base):
    atom_count, slot_width, band_total = raw_proj.shape
    slot_index = jnp.arange(slot_width, dtype=jnp.int32)
    live_slots = (slot_index[None, :] < proj_counts[:, None]).astype(jnp.float32)
    masked = raw_proj * live_slots[:, :, None]
    density = jnp.einsum("apb,aqb->apq", masked * occupations[None, None, :], masked, precision=lax.Precision.HIGHEST) / band_total
    kind_count = onsite_base.shape[0]
    onehot = (species_map[:, None] == jnp.arange(kind_count, dtype=jnp.int32)[None, :]).astype(jnp.float32)
    symmetric = 0.5 * (onsite_base + jnp.swapaxes(onsite_base, 1, 2))
    base_here = jnp.dot(onehot, symmetric.reshape(kind_count, slot_width * slot_width), precision=lax.Precision.HIGHEST).reshape(atom_count, slot_width, slot_width)
    onsite = base_here + hubbard_weight * density
    weighted = jnp.einsum("apq,aqb->apb", onsite, masked, precision=lax.Precision.HIGHEST) * live_slots[:, :, None]
    return masked, weighted


def reference(wave_coeffs, projectors, miller_index, occupations, species_map, proj_counts, onsite_base):
    kinetic = kinetic_of(miller_index)
    current = wave_coeffs
    updated = wave_coeffs.astype(jnp.float32)
    for turn_index in range(ITERS):
        values = current.astype(jnp.float32)
        intersections = lax.dot_general(projectors, current, (((1,), (1,)), ((), ())), preferred_element_type=jnp.float32)
        raw_proj = intersections.reshape(ATOMS, PMAX, BANDS)
        masked, weighted = onsite_apply(raw_proj, occupations, species_map, proj_counts, onsite_base)
        weight_bf = weighted.reshape(ATOMS * PMAX, BANDS).astype(jnp.bfloat16)
        nonlocal_part = lax.dot_general(weight_bf, projectors, (((0,), (0,)), ((), ())), preferred_element_type=jnp.float32)
        applied = kinetic[None, :] * values + nonlocal_part
        norm_sq = jnp.sum(values * values, axis=1)
        kin_sum = jnp.sum(kinetic[None, :] * values * values, axis=1)
        energy_sum = jnp.sum(values * applied, axis=1)
        eigen_value = energy_sum / norm_sq
        band_kinetic = kin_sum / norm_sq
        residual = applied - eigen_value[:, None] * values
        updated = values - step_length * teter_factor(kinetic, band_kinetic) * residual
        if turn_index + 1 < ITERS:
            current = updated.astype(jnp.bfloat16)
    return updated
```

```python
import functools

import jax
import jax.numpy as jnp
from jax import lax
from jax.experimental import pallas as pl
from jax.experimental.pallas import tpu as pltpu
from jax.sharding import PartitionSpec as P

PMAX = 8
ITERS = 2
KINETIC_UNIT = 1.0 / 600.0
HUBBARD = 2.0
STEP = 0.5
MESH = pl.DeviceIdType.MESH
HIGH = lax.Precision.HIGHEST
F32, BF16 = jnp.float32, jnp.bfloat16

SIDE = 4
CHIPS = SIDE * SIDE
OWN = 32
HALF = CHIPS * OWN
PART = HALF // 2
LANES = 256
COLS = 1024
DEPTH = 512


def hops(step):
    return min(step, SIDE - step)


STEPS = sorted(
    ((dy, dx) for dy in range(SIDE) for dx in range(SIDE)), key=lambda s: -(hops(s[0]) + hops(s[1]))
)
BACK = [STEPS.index(((-dy) % SIDE, (-dx) % SIDE)) for dy, dx in STEPS]


def pieces(q):
    hi = q.astype(BF16).astype(F32)
    mid = (q - hi).astype(BF16).astype(F32)
    low = q - hi - mid
    return jnp.concatenate([hi, mid, low, jnp.zeros_like(q)], axis=0)


def whole(parts):
    return parts[0:8] + parts[8:16] + parts[16:24]


def columns_of(q, at, band_here):
    t = jnp.concatenate([q, jnp.zeros((120, 128), F32)], axis=0).T
    return jnp.concatenate([t[64:128, at(i) : at(i) + 1] for i in range(band_here // 64)], axis=0)


def kernel(
    z_count,
    band_total,
    wave,
    proj,
    miller_in,
    occ_in,
    species_in,
    counts_in,
    base_in,
    out,
    miller,
    occ,
    species,
    counts,
    base,
    p_v,
    cur,
    nl,
    hf,
    kin,
    norm_acc,
    kin_acc,
    cols,
    sib_send,
    sib_recv,
    send,
    recv,
    z_send,
    z_recv,
    w_all,
    w_t,
    small_sem,
    p_sem,
    cur_sem,
    sib_ssem,
    sib_rsem,
    ssem,
    rsem,
    z_ssem,
    z_rsem,
    w_ssem,
    w_rsem,
    ws_ssem,
    ws_rsem,
):
    gx, gy = lax.axis_index("gx"), lax.axis_index("gy")
    band_here = wave.shape[0]
    waves = wave.shape[1]
    core = lax.rem(gx, 2)
    chip = gx // 2
    cy, cx = chip // SIDE, lax.rem(chip, SIDE)

    def owner(j, which):
        dy, dx = STEPS[j]
        return (lax.rem(cy + dy, SIDE) * SIDE + lax.rem(cx + dx, SIDE)) * 2 + which

    sibling = (chip * 2 + 1 - core, gy)

    wave_copy = pltpu.make_async_copy(wave, cur.at[pl.ds(0, band_here)], cur_sem)
    wave_copy.start()
    small = [
        pltpu.make_async_copy(source, held, small_sem.at[i])
        for i, (source, held) in enumerate(
            [
                (miller_in, miller),
                (species_in, species),
                (counts_in, counts),
                (base_in, base),
                (occ_in, occ),
            ]
        )
    ]
    for copy in small:
        copy.start()

    def load(part):
        which = 1 - core if part < 2 else core
        for i in range(CHIPS // 2):
            j = (part % 2) * (CHIPS // 2) + i
            rows = pl.ds(pl.multiple_of(owner(j, which) * OWN, OWN), OWN)
            pltpu.make_async_copy(
                proj.at[rows], p_v.at[pl.ds(part * PART + i * OWN, OWN)], p_sem.at[part]
            ).start()

    load(0)
    load(1)

    barrier = pltpu.get_barrier_semaphore()
    for j in range(CHIPS - 1):
        pl.semaphore_signal(barrier, inc=1, device_id=(owner(j, core), gy), device_id_type=MESH)
    for d in range(1, z_count):
        pl.semaphore_signal(
            barrier, inc=1, device_id=(gx, lax.rem(gy + d, z_count)), device_id_type=MESH
        )
    pl.semaphore_signal(barrier, inc=1, device_id=sibling, device_id_type=MESH)

    for copy in small:
        copy.wait()
    mi = miller[...].astype(F32)
    kin[...] = jnp.broadcast_to(
        (1.5 * mi[0:1] * mi[0:1] + 1.0 * mi[1:2] * mi[1:2] + 0.5 * mi[2:3] * mi[2:3]) * KINETIC_UNIT,
        kin.shape,
    )
    atoms_own = OWN // PMAX
    first = gx * atoms_own
    row_atom = lax.broadcasted_iota(jnp.int32, (OWN, band_here), 0) // PMAX
    row_slot = lax.broadcasted_iota(jnp.int32, (OWN, band_here), 0) % PMAX
    lane_atom = lax.broadcasted_iota(jnp.int32, (PMAX, OWN), 1) // PMAX
    row_count = jnp.zeros((OWN, band_here), jnp.int32)
    lane_kind = jnp.zeros((PMAX, OWN), jnp.int32)
    for a in range(atoms_own):
        row_count = jnp.where(row_atom == a, counts[first + a], row_count)
        lane_kind = jnp.where(lane_atom == a, species[first + a], lane_kind)
    live = (row_slot < row_count).astype(F32)
    base_own = jnp.zeros((PMAX, OWN), F32)
    for s in range(base.shape[0]):
        symmetric = 0.5 * (base[s] + base[s].T)
        base_own = jnp.where(
            lane_kind == s, jnp.concatenate([symmetric] * atoms_own, axis=1), base_own
        )
    same_atom = (
        lax.broadcasted_iota(jnp.int32, (OWN, OWN), 0) // PMAX
        == lax.broadcasted_iota(jnp.int32, (OWN, OWN), 1) // PMAX
    )
    lane = lax.broadcasted_iota(jnp.int32, (64, 128), 1)

    def add_norms(values, kin_tile):
        width = values.shape[1]
        sq = values * values
        ksq = kin_tile * sq
        n_part, k_part = sq[:, 0:128], ksq[:, 0:128]
        for i in range(1, width // 128):
            n_part = n_part + sq[:, i * 128 : (i + 1) * 128]
            k_part = k_part + ksq[:, i * 128 : (i + 1) * 128]
        norm_acc[...] += n_part
        kin_acc[...] += k_part

    def zero_norms():
        norm_acc[...] = jnp.zeros_like(norm_acc)
        kin_acc[...] = jnp.zeros_like(kin_acc)

    def packed_norms():
        stack = jnp.zeros((64, 128), F32)
        for i in range(band_here // 64):
            rows = slice(64 * i, 64 * i + 64)
            stack = jnp.where(lane == 2 * i, norm_acc[rows].sum(axis=1, keepdims=True), stack)
            stack = jnp.where(lane == 2 * i + 1, kin_acc[rows].sum(axis=1, keepdims=True), stack)
        return jnp.concatenate([jnp.zeros((64, 128), F32), stack], axis=0).T[0:8]

    cur[pl.ds(band_here, LANES - band_here)] = jnp.zeros((LANES - band_here, waves), BF16)
    wave_copy.wait()
    zero_norms()

    def first_norms(t, _):
        tile = pl.ds(pl.multiple_of(t * DEPTH, DEPTH), DEPTH)
        add_norms(cur[pl.ds(0, band_here), tile].astype(F32), kin[0:1, tile])
        return 0

    lax.fori_loop(0, waves // DEPTH, first_norms, 0)

    for it in range(ITERS):
        last = it == ITERS - 1

        def intersect(part):
            return lax.dot_general(
                p_v[pl.ds(part * PART, PART)],
                cur[...],
                (((1,), (1,)), ((), ())),
                preferred_element_type=F32,
            )

        def load_wait(part):
            if it == 0:
                rows = p_v.at[pl.ds(part * PART, PART)]
                pltpu.make_async_copy(rows, rows, p_sem.at[part]).wait()
                if part < 2:
                    load(part + 2)

        own_norms = packed_norms()
        sib_copies = []
        for part in range(2):
            load_wait(part)
            sums = intersect(part)
            rows = pl.ds(part * PART, PART)
            sib_send[it, rows, 0:128] = sums[:, 0:128].astype(BF16)
            sib_send[it, rows, 128:256] = sums[:, 128:256].astype(BF16)
            if part == 0:
                sib_send[it, pl.ds(0, OWN), 128:256] = (sums[0:OWN, 128:256] + pieces(own_norms)).astype(BF16)
            if it == 0 and part == 0:
                pl.semaphore_wait(barrier, CHIPS - 1 + z_count - 1 + 1)
            copy = pltpu.make_async_remote_copy(
                sib_send.at[it, rows],
                sib_recv.at[it, rows],
                sib_ssem.at[it, part],
                sib_rsem.at[it, part],
                device_id=sibling,
                device_id_type=MESH,
            )
            copy.start()
            sib_copies.append(copy)
        sends = []
        for part in range(2):
            load_wait(2 + part)
            sums = intersect(2 + part)
            rows = pl.ds(part * PART, PART)
            sib_copies[part].wait_recv()
            both = sums + sib_recv[it, rows].astype(F32)
            if part == 0:
                pair_norms = own_norms + whole(sib_recv[it, pl.ds(0, OWN), 128:256].astype(F32))
                pair_pieces = jnp.where(
                    lax.broadcasted_iota(jnp.int32, (OWN, 128), 1) >= 64, pieces(pair_norms), 0.0
                )
            tail = jnp.where(
                lax.broadcasted_iota(jnp.int32, (PART, 128), 1) < 64, both[:, 128:256], 0.0
            ) + jnp.concatenate([pair_pieces] * (PART // OWN), axis=0)
            send[it, rows, 0:128] = both[:, 0:128].astype(BF16)
            send[it, rows, 128:256] = tail.astype(BF16)
            for i in range(CHIPS // 2):
                j = part * (CHIPS // 2) + i
                if j < CHIPS - 1:
                    pltpu.make_async_remote_copy(
                        send.at[it, pl.ds(j * OWN, OWN)],
                        recv.at[it, pl.ds(j * OWN, OWN)],
                        ssem.at[it],
                        rsem.at[it],
                        device_id=(owner(j, core), gy),
                        device_id_type=MESH,
                    ).start()
            if part == 1:
                own_head = both[PART - OWN : PART, 0:128]
                own_tail = both[PART - OWN : PART, 128:256]
        pltpu.make_async_copy(recv.at[it], recv.at[it], rsem.at[it]).wait()
        head = own_head
        tail = jnp.where(
            lax.broadcasted_iota(jnp.int32, (OWN, 128), 1) >= 64, pieces(pair_norms), own_tail
        )
        for j in range(CHIPS - 1):
            rows = pl.ds(j * OWN, OWN)
            head = head + recv[it, rows, 0:128].astype(F32)
            tail = tail + recv[it, rows, 128:256].astype(F32)
        masked = jnp.concatenate([head, tail[:, 0 : band_here - 128]], axis=1) * live

        dense = lax.dot_general(
            masked,
            masked * occ[...],
            (((1,), (1,)), ((), ())),
            preferred_element_type=F32,
            precision=HIGH,
        )
        dense = jnp.where(same_atom, dense, 0.0)
        mine = dense[0:8] + dense[8:16] + dense[16:24] + dense[24:32]
        z_send[it, :, 0:OWN] = mine
        for d in range(1, z_count):
            pltpu.make_async_remote_copy(
                z_send.at[it],
                z_recv.at[it, d - 1],
                z_ssem.at[it],
                z_rsem.at[it],
                device_id=(gx, lax.rem(gy + d, z_count)),
                device_id_type=MESH,
            ).start()

        total = whole(tail)
        norm_col = columns_of(total, lambda i: 2 * i, band_here)
        kin_col = columns_of(total, lambda i: 2 * i + 1, band_here)
        inverse = norm_col / kin_col

        cols[0] = jnp.broadcast_to(inverse, (band_here, 128))

        def factors(t, _):
            tile = pl.ds(pl.multiple_of(t * 128, 128), 128)
            x = kin[0:1, tile] * cols[0]
            n = 27.0 + x * (18.0 + x * (12.0 + 8.0 * x))
            x2 = x * x
            hf[:, tile] = STEP * (n / (n + 16.0 * (x2 * x2)))
            return 0

        lax.fori_loop(0, waves // 128, factors, 0)

        pltpu.make_async_copy(z_recv.at[it], z_recv.at[it], z_rsem.at[it]).wait()
        for d in range(z_count - 1):
            mine = mine + z_recv[it, d, :, 0:OWN]
        onsite = base_own + HUBBARD * (mine / band_total)
        blocks = jnp.where(same_atom, jnp.concatenate([onsite] * atoms_own, axis=0), 0.0)
        weighted = (
            lax.dot_general(
                blocks,
                masked,
                (((0,), (0,)), ((), ())),
                preferred_element_type=F32,
                precision=HIGH,
            )
            * live
        )
        rounded = weighted.astype(BF16).astype(F32)
        energy = jnp.sum(rounded * masked, axis=0, keepdims=True)
        e_head, e_tail = energy[:, 0:128], energy[:, 128:band_here]
        e_tail = jnp.concatenate([e_tail, jnp.zeros((1, 256 - band_here), F32)], axis=1)
        row = lax.broadcasted_iota(jnp.int32, (8, 128), 0)
        e_rows = jnp.where(row == 0, pltpu.roll(jnp.broadcast_to(e_head, (8, 128)), 64, 1), 0.0)
        e_rows = jnp.where(row == 1, jnp.broadcast_to(e_head, (8, 128)), e_rows)
        e_rows = jnp.where(row == 2, pltpu.roll(jnp.broadcast_to(e_tail, (8, 128)), 64, 1), e_rows)
        w_tail = jnp.concatenate(
            [rounded[:, 128:band_here], jnp.zeros((OWN, 256 - band_here), F32)], axis=1
        )
        w_tail = jnp.where(
            lax.broadcasted_iota(jnp.int32, (OWN, 128), 1) >= 64, pieces(e_rows), w_tail
        )
        own_rows = pl.ds(2 * HALF - OWN, OWN)
        w_all[it, own_rows, 0:128] = rounded[:, 0:128].astype(BF16)
        w_all[it, own_rows, 128:256] = w_tail.astype(BF16)
        for j in range(CHIPS - 1):
            pltpu.make_async_remote_copy(
                w_all.at[it, own_rows],
                w_all.at[it, pl.ds(HALF + BACK[j] * OWN, OWN)],
                w_ssem.at[it],
                w_rsem.at[it, BACK[j] // (CHIPS // 2)],
                device_id=(owner(j, core), gy),
                device_id_type=MESH,
            ).start()

        def arrived(part):
            come = w_all.at[it, pl.ds(HALF + part * PART, PART if part == 0 else PART - OWN)]
            pltpu.make_async_copy(come, come, w_rsem.at[it, part]).wait()

        def forward(part):
            copy = pltpu.make_async_remote_copy(
                w_all.at[it, pl.ds(HALF + part * PART, PART)],
                w_all.at[it, pl.ds(part * PART, PART)],
                ws_ssem.at[it, part],
                ws_rsem.at[it, part],
                device_id=sibling,
                device_id_type=MESH,
            )
            copy.start()
            return copy

        def turn(quarter):
            w_t[:, quarter * PART : (quarter + 1) * PART] = w_all[
                it, pl.ds(quarter * PART, PART), 0:band_here
            ].T

        def product(low, high, tile):
            return jnp.dot(
                w_t[:, low * PART : high * PART],
                p_v[pl.ds(low * PART, (high - low) * PART), tile],
                preferred_element_type=F32,
            )

        arrived(1)
        near = forward(1)
        turn(3)

        def own_near(t, _):
            tile = pl.ds(pl.multiple_of(t * COLS, COLS), COLS)
            nl[:, tile] = product(3, 4, tile)
            return 0

        lax.fori_loop(0, waves // COLS, own_near, 0, unroll=True)
        arrived(0)
        far = forward(0)
        turn(2)
        near.wait_recv()
        turn(1)

        def middle(t, _):
            tile = pl.ds(pl.multiple_of(t * COLS, COLS), COLS)
            nl[:, tile] += product(1, 3, tile)
            return 0

        lax.fori_loop(0, waves // COLS, middle, 0, unroll=True)
        far.wait_recv()
        turn(0)
        parts = w_all[it, pl.ds(0, OWN), 128:256].astype(F32)
        for i in range(1, 2 * CHIPS):
            parts = parts + w_all[it, pl.ds(i * OWN, OWN), 128:256].astype(F32)
        energy_col = columns_of(whole(parts), lambda i: i, band_here)
        eigen = (kin_col + energy_col) / norm_col
        cols[1] = jnp.broadcast_to(eigen, (band_here, 128))
        zero_norms()

        def update(t, _):
            tile = pl.ds(pl.multiple_of(t * COLS, COLS), COLS)
            nonlocal_part = nl[:, tile] + product(0, 1, tile)
            v = cur[pl.ds(0, band_here), tile].astype(F32)
            shift = kin[0:1, tile] - jnp.concatenate([cols[1]] * (COLS // 128), axis=1)
            u = v - hf[:, tile] * (nonlocal_part + shift * v)
            if last:
                out[:, tile] = u
            else:
                new = u.astype(BF16)
                cur[pl.ds(0, band_here), tile] = new
                add_norms(new.astype(F32), kin[0:1, tile])
            return 0

        lax.fori_loop(0, waves // COLS, update, 0, unroll=True)

        for part in range(2):
            sib_copies[part].wait_send()
        gone = send.at[it, pl.ds(0, HALF - OWN)]
        pltpu.make_async_copy(gone, gone, ssem.at[it]).wait()
        pltpu.make_async_copy(z_recv.at[it], z_recv.at[it], z_ssem.at[it]).wait()
        gone = w_all.at[it, pl.ds(HALF, HALF - OWN)]
        pltpu.make_async_copy(gone, gone, w_ssem.at[it]).wait()
        near.wait_send()
        far.wait_send()


def local(wave, proj, miller, occ, species, counts, base):
    bands, waves = wave.shape
    slots = proj.shape[0]
    z_count = lax.axis_size("gy")
    hbm = pl.BlockSpec(memory_space=pltpu.HBM)
    dma = pltpu.SemaphoreType.DMA
    return pl.pallas_call(
        functools.partial(kernel, z_count, bands * z_count),
        out_shape=jax.ShapeDtypeStruct((bands, waves), F32),
        in_specs=[hbm] * 7,
        out_specs=pl.BlockSpec(memory_space=pltpu.VMEM),
        scratch_shapes=[
            pltpu.VMEM(miller.shape, jnp.int32),
            pltpu.VMEM((1, bands), F32),
            pltpu.SMEM(species.shape, jnp.int32),
            pltpu.SMEM(counts.shape, jnp.int32),
            pltpu.VMEM(base.shape, F32),
            pltpu.VMEM((slots, waves), BF16),
            pltpu.VMEM((LANES, waves), BF16),
            pltpu.VMEM((bands, waves), F32),
            pltpu.VMEM((bands, waves), F32),
            pltpu.VMEM((8, waves), F32),
            pltpu.VMEM((bands, 128), F32),
            pltpu.VMEM((bands, 128), F32),
            pltpu.VMEM((2, bands, 128), F32),
            pltpu.VMEM((ITERS, HALF, LANES), BF16),
            pltpu.VMEM((ITERS, HALF, LANES), BF16),
            pltpu.VMEM((ITERS, HALF, LANES), BF16),
            pltpu.VMEM((ITERS, HALF - OWN, LANES), BF16),
            pltpu.VMEM((ITERS, 8, 128), F32),
            pltpu.VMEM((ITERS, z_count - 1, 8, 128), F32),
            pltpu.VMEM((ITERS, 2 * HALF, LANES), BF16),
            pltpu.VMEM((bands, 2 * HALF), BF16),
            dma((5,)),
            dma((4,)),
            dma,
            dma((ITERS, 2)),
            dma((ITERS, 2)),
            dma((ITERS,)),
            dma((ITERS,)),
            dma((ITERS,)),
            dma((ITERS,)),
            dma((ITERS,)),
            dma((ITERS, 2)),
            dma((ITERS, 2)),
            dma((ITERS, 2)),
        ],
        compiler_params=pltpu.CompilerParams(
            collective_id=1, has_side_effects=True, vmem_limit_bytes=36 * 2**20
        ),
        name="residual_updates",
    )(*[
        pltpu.with_memory_space_constraint(a, pltpu.HBM)
        for a in (wave, proj, miller, occ[None, :], species, counts, base)
    ])


def solution(mesh):
    placed = (P("gy", "gx"), P(None, "gx"), P(None, "gx"), P("gy"), P(), P(), P())
    return jax.shard_map(
        local, mesh=mesh, in_specs=placed, out_specs=P("gy", "gx"), check_vma=False
    )
```
